512 devices in a mesh: dp: 16 (over x, z_lo), sp: 32 (over z_hi, y, core).
Axes of the slice: x: 4, y: 4, z: 16 (z_hi: 4, z_lo: 4; z = z_hi * 4 + z_lo), core: 2. Of those that a mesh axis runs over, the one named last changes fastest.
Arguments:
- hidden: bfloat16 [16, 4096, 2048], P('dp', 'sp'), may hold values from -6 to 6
- queries: bfloat16 [16, 4096, 2048], P('dp', 'sp'), may hold values from -160 to 160
- key_states: bfloat16 [16, 4096, 512], P('dp', 'sp'), may hold values from -4 to 4
- upstream: bfloat16 [16, 4096, 2048], P('dp', 'sp'), may hold values from -6 to 6
- value_weight: bfloat16 [2048, 512], P('dp'), may hold values from -0.125 to 0.125
- doc_ids: int32 [16, 4096], P('dp', 'sp'), may hold values from 0 to 7, never falling along the last dimension, each value on 1 to 2048 neighbouring positions
Outputs:
- attn_out: bfloat16 [16, 4096, 2048], P('dp', 'sp')
- grad_hidden: bfloat16 [16, 4096, 2048], P('dp', 'sp')
- grad_weight: float32 [2048, 512], P(('dp', 'sp'))
The draws below stay inside these ranges and needn't reach their ends.
Inputs may be any that keep to these rules, and one draw needn't show every extreme that they name: `doc_ids`: never falling along a sequence; each document has 1 to 2048 positions, one exactly 2048.
All inputs are finite; a program needn't handle non-finite values.
Results may differ from the reference program's by a relative error of at most 0.015.
Values may be sent and summed in bfloat16 or wider, within the bound.
No kernel may reach another device: no remote copies, remote signals or barrier semaphores. Data moves between devices by JAX's collectives and lax.ppermute only.
A program may use at most 64 MiB of HBM per device.

```python
import math
import jax
import jax.numpy as jnp
import numpy as np
from jax import lax

D = 2048
H = 32
KVH = 8
HD = 64
BATCH = 16
SEQ = 4096
QD = 2048
KVD = 512


def shared_keys(key):
    return jnp.clip(jax.random.normal(key, (BATCH, SEQ, KVH * HD), jnp.float32), -4.0, 4.0)


def draw_key_states(key, part):
    base_rows = shared_keys(key)
    return base_rows.astype(jnp.bfloat16)


def draw_queries(key, part):
    key = jax.random.fold_in(key, 23)
    fresh = jnp.clip(jax.random.normal(key, (BATCH, SEQ, H * HD), jnp.float32), -4.0, 4.0)
    return fresh.astype(jnp.bfloat16)


def levels(own_key, dims, split, low, top_value):
    factor_of = 1.0
    for position, blocks in split:
        steps = jax.random.uniform(jax.random.fold_in(jax.random.fold_in(own_key, 6), position), (blocks,), jnp.float32, low / len(split), top_value / len(split))
        factor_of = factor_of * jnp.repeat(jnp.exp(steps), dims[position] // blocks).reshape((-1,) + (1,) * (len(dims) - 1 - position))
    return factor_of


def length_profile(number_of, total, limit, skew):
    portions = [(1 << 20) // math.isqrt(rank ** skew) + 1 for rank in range(2, number_of + 1)]
    rest, counts = total - limit - (number_of - 1), [1] * (number_of - 1)
    while rest > 0:
        movable = [i for i in range(number_of - 1) if counts[i] < limit]
        whole, budget = sum([portions[i] for i in movable]), rest
        for i in movable:
            more = min(limit - counts[i], max(1, budget * portions[i] // whole), rest)
            counts[i] = counts[i] + more
            rest = rest - more
    return np.array([limit] + counts)


def uneven(key, count, total, bound, skew):
    if count == 2:
        one = jax.random.randint(key, (), max(1, total - bound), min(bound, total - 1) + 1)
        return jnp.stack([one, total - one])
    lengths = jnp.asarray(length_profile(count, total, bound, skew), jnp.int32)
    pairs = (count - 1) // 2
    donor, sink = lengths[1:1 + 2 * pairs:2], lengths[2:2 + 2 * pairs:2]
    margin = jnp.minimum(donor - 1, bound - sink)
    moved = jax.random.randint(jax.random.fold_in(key, 1), (pairs,), 0, 1 << 20) % (margin + 1)
    lengths = lengths.at[1:1 + 2 * pairs:2].set(donor - moved).at[2:2 + 2 * pairs:2].set(sink + moved)
    return lengths[jax.random.permutation(jax.random.fold_in(key, 2), count)]


def scatter_about(own_key, extent, scale, most, pieces=(), held_as=jnp.bfloat16):
    factor_of = levels(own_key, extent, pieces, -0.22, 0.18) if pieces else 1.0
    entries = jax.random.normal(own_key, extent, jnp.float32) * scale * factor_of
    return jnp.minimum(jnp.maximum(entries, -most), most).astype(held_as)


def setup_inputs(seed: int = 0) -> dict:
    arg_keys = jax.random.split(jax.random.key(seed), 7)
    return {
        "hidden": scatter_about(arg_keys[0], (BATCH, SEQ, D), 1.0, 6.0, ((0, 16), (1, 32))),
        "queries": draw_queries(jax.random.fold_in(arg_keys[6], 71), 0),
        "key_states": draw_key_states(jax.random.fold_in(arg_keys[6], 71), 0),
        "upstream": scatter_about(arg_keys[3], (BATCH, SEQ, QD), 1.0, 6.0, ((0, 16), (1, 32))),
        "value_weight": scatter_about(arg_keys[4], (D, KVD), D ** -0.5, 0.125, ((0, 16),)),
        "doc_ids": jax.vmap(lambda own: jnp.searchsorted(jnp.cumsum(uneven(own, 8, SEQ, SEQ // 2, 0)), jnp.arange(SEQ), side="right"))(jax.random.split(arg_keys[5], BATCH)).reshape((BATCH, SEQ)).astype(jnp.int32),
    }


def head_pass(query_head, key_head, value_head, cotangent_head, allowed):
    score = jnp.dot(query_head, key_head.T, preferred_element_type=jnp.float32) * (1.0 / HD ** 0.5)
    score = jnp.where(allowed, score, jnp.float32(-1e30))
    row_max = jnp.max(score, axis=1, keepdims=True)
    raised = jnp.exp(score - row_max)
    weights_bf = (raised / jnp.sum(raised, axis=1, keepdims=True)).astype(jnp.bfloat16)
    output = jnp.dot(weights_bf, value_head, preferred_element_type=jnp.float32).astype(jnp.bfloat16)
    gradient = jnp.dot(weights_bf.T, cotangent_head, preferred_element_type=jnp.float32).astype(jnp.bfloat16)
    return output, gradient


def reference(hidden, queries, key_states, upstream, value_weight, doc_ids):
    groups = H // KVH

    def one_sequence(inputs):
        hidden_rows, query_rows, key_rows, cotangent_rows, documents = inputs
        seq_len = hidden_rows.shape[0]
        value = jnp.dot(hidden_rows, value_weight, preferred_element_type=jnp.float32).astype(jnp.bfloat16)
        positions = jnp.arange(seq_len, dtype=jnp.int32)
        allowed = (documents[:, None] == documents[None, :]) & (positions[None, :] <= positions[:, None])
        query_heads = query_rows.reshape(seq_len, H, HD).transpose(1, 0, 2)
        cotangent_heads = cotangent_rows.reshape(seq_len, H, HD).transpose(1, 0, 2)
        key_heads = key_rows.reshape(seq_len, KVH, HD).transpose(1, 0, 2)
        value_heads = value.reshape(seq_len, KVH, HD).transpose(1, 0, 2)

        def per_head(head_index):
            group_index = head_index // groups
            return head_pass(query_heads[head_index], key_heads[group_index], value_heads[group_index], cotangent_heads[head_index], allowed)

        outputs, gradients = lax.map(per_head, jnp.arange(H, dtype=jnp.int32))
        attention = outputs.transpose(1, 0, 2).reshape(seq_len, H * HD)
        value_grad = gradients.astype(jnp.float32).reshape(KVH, groups, seq_len, HD).sum(axis=1)
        value_grad = value_grad.astype(jnp.bfloat16).transpose(1, 0, 2).reshape(seq_len, KVH * HD)
        grad_rows = jnp.dot(value_grad, value_weight.T, preferred_element_type=jnp.float32).astype(jnp.bfloat16)
        weight_term = jnp.dot(hidden_rows.T, value_grad, preferred_element_type=jnp.float32)
        return attention, grad_rows, weight_term

    attn_out, grad_hidden, weight_terms = lax.map(one_sequence, (hidden, queries, key_states, upstream, doc_ids))
    return attn_out, grad_hidden, jnp.sum(weight_terms, axis=0)
```

```python
import jax
import jax.numpy as jnp
import numpy as np
from jax import lax
from jax.experimental import pallas as pl
from jax.experimental.pallas import tpu as pltpu
from jax.sharding import Mesh, PartitionSpec as P

D = 2048
H = 32
KVH = 8
HD = 64
GROUPS = H // KVH
TOK = 128
NB = 8
KVD = KVH * HD
WIN = 3 * NB
LANES = GROUPS * TOK
BK = 256
DOCROWS = 16
NEG = -1e30
BF = jnp.bfloat16
F32 = jnp.float32
YC = ("y", "c")
VMEM = 56 * 1024 * 1024


def params(limit=VMEM):
    return pltpu.CompilerParams(vmem_limit_bytes=limit)


def dot(a, b, contract):
    return lax.dot_general(a, b, ((contract[0], contract[1]), ((), ())), preferred_element_type=F32)


def pack_keys_kernel(key_ref, doc_ref, out_ref):
    turned = key_ref[0].T
    docs = jnp.broadcast_to((doc_ref[...] + 1).astype(F32), (DOCROWS, TOK)).astype(BF)
    for g in range(KVH):
        out_ref[g, :HD, :] = turned[g * HD : (g + 1) * HD]
        out_ref[g, HD:, :] = docs


def pack_keys(key_states, doc_ids):
    return pl.pallas_call(
        pack_keys_kernel,
        out_shape=jax.ShapeDtypeStruct((KVH, HD + DOCROWS, TOK), BF),
        name="pack_keys",
        compiler_params=params(),
    )(key_states, doc_ids)


def pack_rows_kernel(query_ref, up_ref, hidden_ref, out_ref):
    part = GROUPS * HD
    row = lax.broadcasted_iota(jnp.int32, (TOK, TOK), 0)
    col = lax.broadcasted_iota(jnp.int32, (TOK, TOK), 1)
    wanted = ((row // 4) % 4) * 32 + (row // 16) * 4 + row % 4
    pick = (col == wanted).astype(F32).astype(BF)
    for g in range(KVH):
        cols = slice(g * part, (g + 1) * part)
        out_ref[g, :part, :] = (query_ref[0, :, cols] * BF(0.125)).T
        out_ref[g, part : 2 * part, :] = up_ref[0, :, cols].T
    for d in range(16):
        moved = dot(pick, hidden_ref[0, :, d * TOK : (d + 1) * TOK], ((1,), (1,))).astype(BF)
        for yc in range(8):
            out_ref[yc, 2 * part + d * 16 : 2 * part + (d + 1) * 16, :] = moved[yc * 16 : (yc + 1) * 16]


def pack_rows(queries, upstream, hidden):
    return pl.pallas_call(
        pack_rows_kernel,
        out_shape=jax.ShapeDtypeStruct((KVH, 3 * GROUPS * HD, TOK), BF),
        name="pack_rows",
        compiler_params=params(),
    )(queries, upstream, hidden)


def first_keys(key_refs):
    docs = [ref[:, HD : HD + 1, :].astype(F32).reshape(NB, TOK) for ref in key_refs]
    starts = []
    for d in range(8):
        total = jnp.zeros((NB, TOK), F32)
        for block in docs:
            total = total + jnp.where(block < d + 1, 1.0, 0.0)
        starts.append(jnp.sum(total))
    own = docs[-1]
    rows = jnp.full((NB, TOK), starts[0], F32)
    for d in range(1, 8):
        rows = jnp.where(own >= d + 1, starts[d], rows)
    return rows.astype(jnp.int32)


def load_keys(key_refs, keys_ref):
    for n, ref in enumerate(key_refs):
        for b in range(NB):
            at = (n * NB + b) * TOK
            keys_ref[at : at + TOK, :] = ref[b, :HD, :].T


def head_lanes(ref, block, offset):
    return jnp.concatenate([ref[block, offset + h * HD : offset + (h + 1) * HD, :] for h in range(GROUPS)], axis=1)


def ranges(start_ref, block):
    row = start_ref[pl.ds(block, 1), :]
    low = jnp.min(row)
    high = jnp.max(row)
    last = (2 * NB + block) // (BK // TOK)
    begin = low // BK
    plain = jnp.minimum((high + BK - 1) // BK, last)
    return jnp.concatenate([row] * GROUPS, axis=1), begin, plain, last


def masked(score, row, tile, block, causal):
    at = tile * BK + lax.broadcasted_iota(jnp.int32, score.shape, 0)
    keep = at >= row
    if causal:
        mine = (2 * NB + block) * TOK + (lax.broadcasted_iota(jnp.int32, score.shape, 1) & (TOK - 1))
        keep = keep & (at <= mine)
    return jnp.where(keep, score, NEG)


def fold(x, op):
    out = x[0:8]
    for i in range(1, x.shape[0] // 8):
        out = op(out, x[i * 8 : i * 8 + 8])
    return out


def grads_kernel(
    far_ref, near_ref, own_ref, rows_ref, out_far, out_near, out_own, lse_ref, keys_ref, start_ref, score_ref, prob_ref, grad_ref
):
    key_refs = (far_ref, near_ref, own_ref)
    load_keys(key_refs, keys_ref)
    start_ref[...] = first_keys(key_refs)
    grad_ref[...] = jnp.zeros_like(grad_ref)

    def one_block(block, _):
        row, begin, plain, last = ranges(start_ref, block)
        query = head_lanes(rows_ref, block, 0)

        def put(tile, high, mode):
            at = pl.multiple_of(tile * BK, BK)
            score = jnp.dot(keys_ref[pl.ds(at, BK), :], query, preferred_element_type=F32)
            if mode:
                score = masked(score, row, tile, block, mode == 2)
            score_ref[pl.ds(at, BK), :] = score
            return jnp.maximum(high, fold(score, jnp.maximum))

        high = jnp.full((8, LANES), NEG, F32)
        high = lax.fori_loop(begin, plain, lambda t, h: put(t, h, 1), high)
        high = lax.fori_loop(plain, last, lambda t, h: put(t, h, 0), high)
        high = put(last, high, 2)
        high = jnp.max(high, axis=0, keepdims=True)

        def raise_(tile, total):
            at = pl.multiple_of(tile * BK, BK)
            raised = jnp.exp(score_ref[pl.ds(at, BK), :] - high)
            prob_ref[pl.ds(at, BK), :] = raised.astype(BF)
            return total + fold(raised, jnp.add)

        total = lax.fori_loop(begin, last + 1, raise_, jnp.zeros((8, LANES), F32))
        total = jnp.sum(total, axis=0, keepdims=True)
        lse_ref[block] = jnp.broadcast_to(high + jnp.log(total), (8, LANES))
        up = (head_lanes(rows_ref, block, GROUPS * HD).astype(F32) * (1.0 / total)).astype(BF)

        def back(tile, _):
            at = pl.multiple_of(tile * BK, BK)
            grad_ref[pl.ds(at, BK), :] += dot(prob_ref[pl.ds(at, BK), :], up, ((1,), (1,)))
            return 0

        lax.fori_loop(begin, last + 1, back, 0)
        return 0

    lax.fori_loop(0, NB, one_block, 0)
    for n, out in enumerate((out_far, out_near, out_own)):
        for b in range(NB):
            at = (n * NB + b) * TOK
            out[b] = grad_ref[at : at + TOK, :].T.astype(out.dtype)


def grads(keys, rows):
    shape = (NB, HD, TOK)
    return pl.pallas_call(
        grads_kernel,
        out_shape=(
            jax.ShapeDtypeStruct(shape, BF),
            jax.ShapeDtypeStruct(shape, BF),
            jax.ShapeDtypeStruct(shape, F32),
            jax.ShapeDtypeStruct((NB, 8, LANES), F32),
        ),
        scratch_shapes=[
            pltpu.VMEM((WIN * TOK, HD), BF),
            pltpu.VMEM((NB, TOK), jnp.int32),
            pltpu.VMEM((WIN * TOK, LANES), F32),
            pltpu.VMEM((WIN * TOK, LANES), BF),
            pltpu.VMEM((WIN * TOK, HD), F32),
        ],
        name="grads",
        compiler_params=params(),
    )(*keys, rows)


def outs_kernel(
    far_ref, near_ref, own_ref, vfar_ref, vnear_ref, vown_ref, rows_ref, lse_ref, out_ref, keys_ref, start_ref, value_ref
):
    key_refs = (far_ref, near_ref, own_ref)
    load_keys(key_refs, keys_ref)
    start_ref[...] = first_keys(key_refs)
    per = BK // TOK
    for n, ref in enumerate((vfar_ref, vnear_ref, vown_ref)):
        for b in range(NB):
            value_ref[(n * NB + b) // per, :, (b % per) * TOK : (b % per + 1) * TOK] = ref[b]

    def one_block(block, _):
        row, begin, plain, last = ranges(start_ref, block)
        query = head_lanes(rows_ref, block, 0)
        lse = lse_ref[block, 0:1, :]

        def add(tile, total, mode):
            at = pl.multiple_of(tile * BK, BK)
            score = jnp.dot(keys_ref[pl.ds(at, BK), :], query, preferred_element_type=F32)
            if mode:
                score = masked(score, row, tile, block, mode == 2)
            probs = jnp.exp(score - lse).astype(BF)
            return total + jnp.dot(value_ref[tile], probs, preferred_element_type=F32)

        total = jnp.zeros((HD, LANES), F32)
        total = lax.fori_loop(begin, plain, lambda t, c: add(t, c, 1), total)
        total = lax.fori_loop(plain, last, lambda t, c: add(t, c, 0), total)
        total = add(last, total, 2).astype(BF)
        for h in range(GROUPS):
            out_ref[block, h * HD : (h + 1) * HD, :] = total[:, h * TOK : (h + 1) * TOK]
        return 0

    lax.fori_loop(0, NB, one_block, 0)


def outs(keys, values, rows, lse):
    return pl.pallas_call(
        outs_kernel,
        out_shape=jax.ShapeDtypeStruct((NB, GROUPS * HD, TOK), BF),
        scratch_shapes=[
            pltpu.VMEM((WIN * TOK, HD), BF),
            pltpu.VMEM((NB, TOK), jnp.int32),
            pltpu.VMEM((WIN * TOK // BK, HD, BK), BF),
        ],
        name="outs",
        compiler_params=params(),
    )(*keys, *values, rows, lse)


def weight_kernel(grad_ref, rows_ref, out_ref, left_ref, right_ref):
    part = GROUPS * HD
    for b in range(NB):
        at = slice(b * TOK, (b + 1) * TOK)
        left_ref[:, at] = rows_ref[b, 2 * part : 3 * part, :]
        for g in range(KVH):
            right_ref[g * HD : (g + 1) * HD, at] = grad_ref[g, b]
    out_ref[...] = dot(left_ref[...], right_ref[...], ((1,), (1,))).astype(BF)


def weight_part(value_grads, rows):
    return pl.pallas_call(
        weight_kernel,
        out_shape=jax.ShapeDtypeStruct((GROUPS * HD, KVD), BF),
        scratch_shapes=[pltpu.VMEM((GROUPS * HD, NB * TOK), BF), pltpu.VMEM((KVD, NB * TOK), BF)],
        name="weight_part",
        compiler_params=params(),
    )(value_grads, rows)


def shift(x, by):
    return lax.ppermute(x, "zh", [(z, z + by) for z in range(4) if 0 <= z + by < 4])


def exchange(x, axes):
    return lax.all_to_all(x, axes, split_axis=0, concat_axis=0, tiled=True)


def body(hidden, queries, key_states, upstream, value_weight, doc_ids):
    core = lax.axis_index("c")
    place = lax.axis_index(YC)
    half = KVD // 2

    key_own = exchange(pack_keys(key_states, doc_ids), YC)
    key_near, key_far = shift(key_own, 1), shift(key_own, 2)
    keys = (key_far, key_near, key_own)

    rows = exchange(pack_rows(queries, upstream, hidden), YC)

    my_half = lax.dynamic_slice_in_dim(value_weight, core * half, half, 1)
    mine = exchange(jnp.broadcast_to(my_half[None], (16, TOK, half)), ("x", "zl")).reshape(D, half)
    other = lax.ppermute(mine, "c", [(0, 1), (1, 0)])
    mine_v = dot(mine, hidden[0], ((0,), (1,))).astype(BF)
    other_v = dot(other, hidden[0], ((0,), (1,))).astype(BF)
    value = jnp.where(core == 0, jnp.concatenate([mine_v, other_v]), jnp.concatenate([other_v, mine_v]))
    value_own = exchange(value.reshape(KVH, HD, TOK), YC)

    grad_far, grad_near, grad_own, lse = grads(keys, rows)
    grad_own = grad_own + shift(grad_near, -1).astype(F32) + shift(grad_far, -2).astype(F32)
    mine_grad = grad_own.astype(BF)
    value_grads = exchange(jnp.broadcast_to(mine_grad[None], (KVH, NB, HD, TOK)), YC)

    value_near, value_far = shift(value_own, 1), shift(value_own, 2)
    out = outs(keys, (value_far, value_near, value_own), rows, lse)
    attn = exchange(out, YC).reshape(D, TOK).T.reshape(1, TOK, D)

    partial = weight_part(value_grads, rows).reshape(64, 4, KVD)
    grad_weight = exchange(partial, ("x", "zl", "zh")).astype(F32).sum(axis=0)

    here = lax.dynamic_index_in_dim(value_grads, place, 1, keepdims=False).reshape(2, half, TOK)
    here_mine = lax.dynamic_index_in_dim(here, core, 0, keepdims=False)
    here_other = lax.dynamic_index_in_dim(here, 1 - core, 0, keepdims=False)
    grad_hidden = dot(here_mine, mine, ((0,), (1,))) + dot(here_other, other, ((0,), (1,)))
    return attn, grad_hidden.astype(BF).reshape(1, TOK, D), grad_weight


def solution(mesh):
    fine = Mesh(np.asarray(mesh.devices).reshape(4, 4, 4, 4, 2), ("x", "zl", "zh", "y", "c"))
    dp, sp = ("x", "zl"), ("zh", "y", "c")
    return jax.shard_map(
        body,
        mesh=fine,
        in_specs=(P(dp, sp, None),) * 4 + (P(dp, None), P(dp, sp)),
        out_specs=(P(dp, sp, None), P(dp, sp, None), P(dp + sp, None)),
        check_vma=False,
    )
```
